32 devices in a mesh: stripe: 8 (over z, core), tile: 4 (over y, x).
Axes of the slice: x: 2, y: 2, z: 4, core: 2. Of those that a mesh axis runs over, the one named last changes fastest.
Arguments:
- positions: int32 [8, 12], P('stripe', 'tile'), may hold values from -64 to -64, as said below
- row_offsets: int32 [8, 12], P('stripe', 'tile'), may hold values from -64 to 64, as said below
- amplitudes: float32 [8, 12, 256, 256], P('stripe', 'tile'), may hold values from 0 to 2
- object_field: float32 [2, 2048, 512], P(None, 'stripe', 'tile'), may hold values from -6 to 6
- probe_field: float32 [2, 256, 256], replicated, may hold values from -6 to 6
Outputs:
- object_out: float32 [2, 2048, 512], P(None, 'stripe', 'tile')
- probe_out: float32 [2, 256, 256], replicated
The draws below stay inside these ranges and needn't reach their ends.
Inputs may be any that keep to these rules, and one draw needn't show every extreme that they name: `positions`: in every block of 3 patterns of one stripe and one tile, the first offset is -64 and the second is 128 - 192. `row_offsets`: in every block of 3 patterns of one stripe and one tile, the first row offset is -64 and the second is 64.
All inputs are finite; a program needn't handle non-finite values.
Results may differ from the reference program's by a relative error of at most 0.0006.
The reference program's roundings to bfloat16 on the way count: a program that leaves them out, or rounds other values in their place, can miss the bound.
Values sent between devices are 32-bit elements; how exact they have to be, the bound alone decides.
A program may use at most 64 MiB of HBM per device.

```python
import math
import jax
import jax.numpy as jnp
from jax import lax

PW = 256
HALO = 64
TILE_W = 128
PAT_DEV = 3
INNER = 2
OUTER = 2
STRIPES = 8
PATTERNS = 12
OH = 2048
OW = 512


def draw_positions(key, part):
    lowest = -HALO
    highest = TILE_W + HALO - PW
    own_key = jax.random.fold_in(key, 3)
    values = jax.random.randint(own_key, (STRIPES, PATTERNS), lowest, highest + 1)
    within = jnp.arange(PATTERNS, dtype=jnp.int32) % PAT_DEV
    values = jnp.where(within[None, :] == 0, lowest, jnp.where(within[None, :] == 1, highest, values))
    return values.astype(jnp.int32)


def draw_row_offsets(key, part):
    own_key = jax.random.fold_in(key, 7)
    values = jax.random.randint(own_key, (STRIPES, PATTERNS), -HALO, HALO + 1)
    within = jnp.arange(PATTERNS, dtype=jnp.int32) % PAT_DEV
    values = jnp.where(within[None, :] == 0, -HALO, jnp.where(within[None, :] == 1, HALO, values))
    return values.astype(jnp.int32)


def levels(key, dims, pieces, low, high):
    def one(axis_at, shards_of):
        heights = jax.random.uniform(jax.random.fold_in(jax.random.fold_in(key, 6), axis_at), (shards_of,), jnp.float32, low / len(pieces), high / len(pieces))
        return jnp.repeat(jnp.exp(heights), dims[axis_at] // shards_of).reshape((-1,) + (1,) * (len(dims) - axis_at - 1))

    loudness = one(*pieces[0])
    for cut in pieces[1:]:
        loudness = loudness * one(*cut)
    return loudness


def noise(key, shape, width, most, split=(), kind=jnp.bfloat16):
    result = jax.random.normal(key, shape, jnp.float32) * width
    if len(split) > 0:
        result = levels(key, shape, split, -0.22, 0.18) * result
    return jnp.clip(result, min=-most, max=most).astype(kind)


def setup_inputs(seed: int = 0) -> dict:
    splits = jax.random.split(jax.random.key(seed), 6)
    positions = draw_positions(jax.random.fold_in(splits[5], 71), 0)
    row_offsets = draw_row_offsets(jax.random.fold_in(splits[5], 71), 0)
    amplitudes = jnp.clip(2.0 * jax.random.uniform(splits[2], (STRIPES, PATTERNS, PW, PW), jnp.float32) ** levels(splits[2], (STRIPES, PATTERNS, PW, PW), ((0, 8), (1, 4)), -0.2, 0.2), 0.0, 2.0)
    object_field = noise(splits[3], (2, OH, OW), 1.0, 6.0, ((1, 8), (2, 4)), jnp.float32)
    probe_field = noise(splits[4], (2, PW, PW), 1.0, 6.0, (), jnp.float32)
    return dict(positions=positions, row_offsets=row_offsets, amplitudes=amplitudes, object_field=object_field, probe_field=probe_field)


def dft_tables():
    indices = jnp.arange(PW, dtype=jnp.int32)
    phase = indices[:, None] * indices[None, :] % PW
    angles = phase.astype(jnp.float32) * (2.0 * math.pi / PW)
    factor = 1.0 / math.sqrt(PW)
    return ((jnp.cos(angles) * factor).astype(jnp.bfloat16), (jnp.sin(angles) * factor).astype(jnp.bfloat16))

def apply_left(matrix, batch):
    return jnp.einsum('kn,pnm->pkm', matrix.astype(jnp.float32), batch.astype(jnp.float32))

def apply_right(batch, matrix):
    return jnp.einsum('pkn,nm->pkm', batch.astype(jnp.float32), matrix.astype(jnp.float32))

def pattern_pass(windows, probe_field, measured, cosine, sine):
    win_re = windows[:, 0]
    win_im = windows[:, 1]
    probe_re = probe_field[0]
    probe_im = probe_field[1]
    exit_re = (probe_re * win_re - probe_im * win_im).astype(jnp.bfloat16)
    exit_im = (probe_re * win_im + probe_im * win_re).astype(jnp.bfloat16)
    half_re = (apply_left(cosine, exit_re) + apply_left(sine, exit_im)).astype(jnp.bfloat16)
    half_im = (apply_left(cosine, exit_im) - apply_left(sine, exit_re)).astype(jnp.bfloat16)
    spec_re = apply_right(half_re, cosine) + apply_right(half_im, sine)
    spec_im = apply_right(half_im, cosine) - apply_right(half_re, sine)
    magnitude = jnp.sqrt(spec_re * spec_re + spec_im * spec_im)
    scaling = measured / jnp.maximum(magnitude, 0.5)
    miss_re = (spec_re - scaling * spec_re).astype(jnp.bfloat16)
    miss_im = (spec_im - scaling * spec_im).astype(jnp.bfloat16)
    hb_re = (apply_left(cosine, miss_re) - apply_left(sine, miss_im)).astype(jnp.bfloat16)
    hb_im = (apply_left(cosine, miss_im) + apply_left(sine, miss_re)).astype(jnp.bfloat16)
    back_re = apply_right(hb_re, cosine) - apply_right(hb_im, sine)
    back_im = apply_right(hb_im, cosine) + apply_right(hb_re, sine)
    object_grad = jnp.stack([probe_re * back_re + probe_im * back_im, probe_re * back_im - probe_im * back_re], axis=1)
    probe_grad = jnp.stack([lax.optimization_barrier(jnp.sum(win_re * back_re + win_im * back_im, axis=0)), lax.optimization_barrier(jnp.sum(win_re * back_im - win_im * back_re, axis=0))])
    illumination = lax.optimization_barrier(jnp.sum(win_re * win_re + win_im * win_im, axis=0))
    return (object_grad, probe_grad, illumination)

def reference(positions, row_offsets, amplitudes, object_field, probe_field):
    cosine, sine = dft_tables()
    padded_width = OW + 2 * HALO
    padded_height = OH + 2 * HALO
    tile_start = jnp.arange(PATTERNS, dtype=jnp.int32) // PAT_DEV * TILE_W
    starts_all = (positions + tile_start[None, :] + HALO).astype(jnp.int32)
    stripe_top = jnp.arange(STRIPES, dtype=jnp.int32) * PW
    rows_all = (row_offsets + stripe_top[:, None] + HALO).astype(jnp.int32)
    zero_index = jnp.zeros((), jnp.int32)
    current = object_field
    for outer_step in range(OUTER):
        grad_sum = jnp.zeros((2, PW, PW), jnp.float32)
        light_sum = jnp.zeros((PW, PW), jnp.float32)
        for inner_step in range(INNER):
            padded = jnp.pad(current, ((0, 0), (HALO, HALO), (HALO, HALO)))
            step_size = 1.0 / (2.0 * PAT_DEV * jnp.max(probe_field[0] * probe_field[0] + probe_field[1] * probe_field[1]) + 1e-06)

            def stripe_pass(carry, stripe):
                starts = starts_all[stripe]
                row_list = rows_all[stripe]
                windows = jax.vmap(lambda row_start, column_start: lax.dynamic_slice(padded, (zero_index, row_start, column_start), (2, PW, PW)))(row_list, starts)
                object_grad, probe_grad, illumination = pattern_pass(windows, probe_field, amplitudes[stripe], cosine, sine)

                def add_one(pattern, total):
                    where = (zero_index, row_list[pattern], starts[pattern])
                    before = lax.dynamic_slice(total, where, (2, PW, PW))
                    return lax.dynamic_update_slice(total, before + object_grad[pattern], where)
                full_total = lax.fori_loop(0, PATTERNS, add_one, carry[2])
                return ((carry[0] + probe_grad, carry[1] + illumination, full_total), None)
            start_carry = (jnp.zeros((2, PW, PW), jnp.float32), jnp.zeros((PW, PW), jnp.float32), jnp.zeros((2, padded_height, padded_width), jnp.float32))
            (grad_sum, light_sum, full_grad), unused = lax.scan(stripe_pass, start_carry, jnp.arange(STRIPES, dtype=jnp.int32))
            current = current - step_size * full_grad[:, HALO:HALO + OH, HALO:HALO + OW]
        probe_field = probe_field - 0.5 * grad_sum / (light_sum + 1.0)
    return (current, probe_field)
```

```python
import functools
import math

import jax
import jax.numpy as jnp
import ml_dtypes
import numpy as np
from jax import lax
from jax.experimental import pallas as pl
from jax.experimental.pallas import tpu as pltpu
from jax.sharding import PartitionSpec as P

HALO = 64
INNER = 2
OUTER = 2
CHUNK = 128


def dft_blocks(size):
    indices = np.arange(size)
    angles = (indices[:, None] * indices[None, :] % size).astype(np.float64) * (2.0 * math.pi / size)
    factor = np.float32(1.0 / math.sqrt(size))
    cosine = (np.cos(angles).astype(np.float32) * factor).astype(ml_dtypes.bfloat16)
    sine = (np.sin(angles).astype(np.float32) * factor).astype(ml_dtypes.bfloat16)
    forward = np.block([[cosine, sine], [-sine, cosine]])
    inverse = np.block([[cosine, -sine], [sine, cosine]])
    return forward, inverse


def dot(a, b):
    return jnp.dot(a, b, preferred_element_type=jnp.float32)


def kernel(
    stripes, tiles, patterns,
    rows_ref, amp_ref, obj_ref, probe_ref, fwd_ref, inv_ref,
    obj_out, probe_out,
    ext, grad, shifted, window, exits, misses, cols, edges, totals, probes,
    pair_in, pair_sum, tile_in, tile_sum, z_in, send_sem, recv_sem,
):
    size = probe_ref.shape[-1]
    own_rows = obj_ref.shape[1]
    s = lax.axis_index("stripe")
    t = lax.axis_index("tile")
    core = lax.rem(s, 2)
    z = s // 2
    pairs = stripes // 2
    lo, hi = HALO, HALO + own_rows
    half_w = size // 2
    used = [0]

    class Copy:
        def __init__(self, src, dst, device, sends=None, receives=None):
            n = used[0]
            used[0] += 1
            self.sends, self.receives = sends, receives
            self.make = lambda: pltpu.make_async_remote_copy(
                src_ref=src, dst_ref=dst, send_sem=send_sem.at[n], recv_sem=recv_sem.at[n],
                device_id=device, device_id_type=pl.DeviceIdType.MESH,
            )

        def start(self):
            self.guard(self.sends, lambda: self.make().start())

        def sent(self):
            self.guard(self.sends, lambda: self.make().wait_send())

        def arrived(self):
            self.guard(self.receives, lambda: self.make().wait_recv())

        def guard(self, condition, act):
            if condition is None:
                act()
            else:
                pl.when(condition)(act)

    left, right = jnp.maximum(t - 1, 0), jnp.minimum(t + 1, tiles - 1)
    above, below = jnp.maximum(s - 1, 0), jnp.minimum(s + 1, stripes - 1)
    has_left, has_right = t > 0, t < tiles - 1
    has_above, has_below = s > 0, s < stripes - 1

    def to_left(src, dst):
        return Copy(src, dst, (s, left), has_left, has_right)

    def to_right(src, dst):
        return Copy(src, dst, (s, right), has_right, has_left)

    def to_above(src, dst):
        return Copy(src, dst, (above, t), has_above, has_below)

    def to_below(src, dst):
        return Copy(src, dst, (below, t), has_below, has_above)

    def column_copies(src, step, first, last):
        return [
            to_left(
                src.at[:, lo + first : lo + last, :half_w], cols.at[step, 1, :, first:last, :]
            ),
            to_right(
                src.at[:, lo + first : lo + last, half_w:], cols.at[step, 0, :, first:last, :]
            ),
        ]

    lane = lax.broadcasted_iota(jnp.int32, (own_rows, half_w), 1)
    ext[:, :lo, :] = jnp.zeros((2, lo, size), jnp.float32)
    ext[:, hi:, :] = jnp.zeros((2, ext.shape[1] - hi, size), jnp.float32)
    for part in range(2):
        turned = pltpu.roll(obj_ref[part], HALO, 1)
        ext[part, lo:hi, :half_w] = jnp.where(lane >= HALO, turned, 0.0)
        ext[part, lo:hi, half_w:] = jnp.where(lane < HALO, turned, 0.0)
    probes[0] = probe_ref[...]

    barrier = pltpu.get_barrier_semaphore()

    def greet(device):
        pl.semaphore_signal(barrier, inc=1, device_id=device, device_id_type=pl.DeviceIdType.MESH)

    for k in range(1, tiles):
        greet((s, lax.rem(t + k, tiles)))
    for k in range(1, pairs):
        greet((lax.rem(z + k, pairs) * 2 + core, t))
    pl.when(has_above)(lambda: greet((above, t)))
    pl.when(has_below)(lambda: greet((below, t)))
    pl.semaphore_wait(
        barrier,
        tiles - 1 + pairs - 1 + has_above.astype(jnp.int32) + has_below.astype(jnp.int32),
    )

    first = column_copies(ext, 0, 0, own_rows)
    for copy in first:
        copy.start()
    pad = 4 * HALO
    shifted[:, : pad // 2, :] = jnp.zeros((2, pad // 2, size), jnp.float32)
    shifted[:, pad // 2 + size :, :] = jnp.zeros((2, pad // 2 , size), jnp.float32)
    for copy in first:
        copy.sent()
        copy.arrived()

    @pl.when(has_left)
    def _():
        ext[:, lo:hi, :half_w] += cols[0, 0]

    @pl.when(has_right)
    def _():
        ext[:, lo:hi, half_w:] += cols[0, 1]

    def row_halo():
        return [
            to_above(ext.at[:, lo : lo + HALO, :], ext.at[:, hi : hi + HALO, :]),
            to_below(ext.at[:, hi - HALO : hi, :], ext.at[:, :lo, :]),
        ]

    halo = row_halo()
    for copy in halo:
        copy.start()
    for copy in halo:
        copy.arrived()
    for copy in halo:
        copy.sent()

    offset = rows_ref[0, patterns - 1] + HALO

    def rows_from(source, start, target):
        length = target.shape[1]
        total = source.shape[1]
        for part in range(2):
            for c in range(0, size, half_w):
                block = source[part, :, c : c + half_w]
                for bit in reversed(range((2 * HALO).bit_length())):
                    turned = pltpu.roll(block, total - (1 << bit), 0)
                    block = jnp.where(((start >> bit) & 1) == 1, turned, block)
                target[part, :, c : c + half_w] = block[:length]

    def pattern_pass(index, source, top, probe, target, base, accumulate, totals_mode):
        for r in range(0, size, CHUNK):
            w_re = source[0, top + r : top + r + CHUNK, :]
            w_im = source[1, top + r : top + r + CHUNK, :]
            p_re = probe[0, r : r + CHUNK, :]
            p_im = probe[1, r : r + CHUNK, :]
            exits[r : r + CHUNK, :] = (p_re * w_re - p_im * w_im).astype(jnp.bfloat16)
            exits[size + r : size + r + CHUNK, :] = (p_re * w_im + p_im * w_re).astype(jnp.bfloat16)
        for r in range(0, size, CHUNK):
            h_re = dot(fwd_ref[r : r + CHUNK, :], exits[...]).astype(jnp.bfloat16)
            h_im = dot(fwd_ref[size + r : size + r + CHUNK, :], exits[...]).astype(jnp.bfloat16)
            spec = dot(jnp.concatenate([h_re, h_im], axis=1), inv_ref[...])
            s_re, s_im = spec[:, :size], spec[:, size:]
            power = jnp.maximum(s_re * s_re + s_im * s_im, 0.25)
            scaling = amp_ref[0, index, r : r + CHUNK, :] * lax.rsqrt(power)
            misses[r : r + CHUNK, :] = (s_re - scaling * s_re).astype(jnp.bfloat16)
            misses[size + r : size + r + CHUNK, :] = (s_im - scaling * s_im).astype(jnp.bfloat16)
        for r in range(0, size, CHUNK):
            h_re = dot(inv_ref[r : r + CHUNK, :], misses[...]).astype(jnp.bfloat16)
            h_im = dot(inv_ref[size + r : size + r + CHUNK, :], misses[...]).astype(jnp.bfloat16)
            back = dot(jnp.concatenate([h_re, h_im], axis=1), fwd_ref[...])
            b_re, b_im = back[:, :size], back[:, size:]
            p_re = probe[0, r : r + CHUNK, :]
            p_im = probe[1, r : r + CHUNK, :]
            g_re = p_re * b_re + p_im * b_im
            g_im = p_re * b_im - p_im * b_re
            where = slice(base + r, base + r + CHUNK)
            if accumulate:
                g_re = g_re + target[0, where, :]
                g_im = g_im + target[1, where, :]
            target[0, where, :] = g_re
            target[1, where, :] = g_im
            if totals_mode is not None:
                w_re = source[0, top + r : top + r + CHUNK, :]
                w_im = source[1, top + r : top + r + CHUNK, :]
                q_re = w_re * b_re + w_im * b_im
                q_im = w_re * b_im - w_im * b_re
                light = w_re * w_re + w_im * w_im
                if totals_mode:
                    q_re = q_re + totals[0, r : r + CHUNK, :]
                    q_im = q_im + totals[1, r : r + CHUNK, :]
                    light = light + totals[2, r : r + CHUNK, :]
                totals[0, r : r + CHUNK, :] = q_re
                totals[1, r : r + CHUNK, :] = q_im
                totals[2, r : r + CHUNK, :] = light

    half_rows = size // 2
    tile_rows = half_rows // tiles
    z_rows = tile_rows // pairs
    scatter_z = z_rows >= 8 and z_rows * pairs == tile_rows

    for outer in range(OUTER):
        probe = probes.at[outer]
        fresh = probes.at[outer + 1]
        p_re, p_im = probe[0], probe[1]
        step_size = 1.0 / (2.0 * patterns * jnp.max(p_re * p_re + p_im * p_im) + 1e-06)
        for inner in range(INNER):
            step = outer * INNER + inner
            last_inner = inner == INNER - 1
            final = last_inner and outer == OUTER - 1
            rows_from(ext, offset, window)
            mode = (lambda later: later) if last_inner else (lambda later: None)
            pattern_pass(patterns - 1, window, 0, probe, shifted, pad // 2, False, mode(False))
            rows_from(shifted, 2 * HALO - offset, grad)
            pattern_pass(0, ext, 0, probe, grad, 0, True, mode(True))
            up = to_above(grad.at[:, :lo, :], edges.at[step, 1])
            up.start()
            pattern_pass(1, ext, 2 * HALO, probe, grad, 2 * HALO, True, mode(True))
            down = to_below(grad.at[:, hi:, :], edges.at[step, 0])
            down.start()
            middle = column_copies(grad, step + 1, HALO, own_rows - HALO)
            for copy in middle:
                copy.start()
            if last_inner:
                pair = Copy(
                    totals.at[:, pl.ds(pl.multiple_of((1 - core) * half_rows, half_rows), half_rows), :],
                    pair_in.at[outer],
                    (s + 1 - 2 * core, t),
                )
                pair.start()
            down.arrived()

            @pl.when(has_above)
            def _():
                grad[:, lo : lo + HALO, :] += edges[step, 0]

            upper = column_copies(grad, step + 1, 0, HALO)
            for copy in upper:
                copy.start()
            up.arrived()

            @pl.when(has_below)
            def _():
                grad[:, hi - HALO : hi, :] += edges[step, 1]

            lower = column_copies(grad, step + 1, own_rows - HALO, own_rows)
            for copy in lower:
                copy.start()

            if last_inner:
                pair.arrived()
                kept = pl.ds(pl.multiple_of(core * half_rows, half_rows), half_rows)
                pair_sum[...] = totals[:, kept, :] + pair_in[outer]
                over_tiles = []
                for k in range(1, tiles):
                    to = lax.rem(t + k, tiles)
                    over_tiles.append(
                        Copy(
                            pair_sum.at[:, pl.ds(pl.multiple_of(to * tile_rows, tile_rows), tile_rows), :],
                            tile_in.at[outer, k - 1],
                            (s, to),
                        )
                    )
                    over_tiles[-1].start()

            outside_left = jnp.logical_and(jnp.logical_not(has_left), lane < HALO)
            outside_right = jnp.logical_and(jnp.logical_not(has_right), lane >= HALO)
            for part in range(2):
                ext[part, lo:hi, :half_w] -= jnp.where(
                    outside_left, 0.0, step_size * grad[part, lo:hi, :half_w]
                )
                ext[part, lo:hi, half_w:] -= jnp.where(
                    outside_right, 0.0, step_size * grad[part, lo:hi, half_w:]
                )
            for copy in middle + upper + lower:
                copy.arrived()

            @pl.when(has_left)
            def _():
                ext[:, lo:hi, :half_w] -= step_size * cols[step + 1, 0]

            @pl.when(has_right)
            def _():
                ext[:, lo:hi, half_w:] -= step_size * cols[step + 1, 1]

            if not final:
                halo = row_halo()
                for copy in halo:
                    copy.start()
            else:
                halo = []
                for part in range(2):
                    obj_out[part] = jnp.where(
                        lane < HALO,
                        pltpu.roll(ext[part, lo:hi, :half_w], HALO, 1),
                        pltpu.roll(ext[part, lo:hi, half_w:], HALO, 1),
                    )

            if last_inner:
                for copy in over_tiles:
                    copy.arrived()
                mine = pl.ds(pl.multiple_of(t * tile_rows, tile_rows), tile_rows)
                total = pair_sum[:, mine, :]
                for k in range(tiles - 1):
                    total = total + tile_in[outer, k]
                tile_sum[...] = total
                over_z = []
                for k in range(1, pairs):
                    to = lax.rem(z + k, pairs)
                    if scatter_z:
                        piece = pl.ds(pl.multiple_of(to * z_rows, z_rows), z_rows)
                        source = tile_sum.at[:, piece, :]
                    else:
                        source = tile_sum
                    over_z.append(Copy(source, z_in.at[outer, k - 1], (to * 2 + core, t)))
                    over_z[-1].start()
                for copy in over_z:
                    copy.arrived()
                start_row = core * half_rows + t * tile_rows
                if scatter_z:
                    total = tile_sum[:, pl.ds(pl.multiple_of(z * z_rows, z_rows), z_rows), :]
                    count = z_rows
                    new_row = start_row + z * z_rows
                else:
                    total = tile_sum[...]
                    count = tile_rows
                    new_row = start_row
                for k in range(pairs - 1):
                    total = total + z_in[outer, k]
                place = pl.ds(pl.multiple_of(new_row, count), count)
                fresh[:, place, :] = probe[:, place, :] - 0.5 * total[:2] / (total[2:] + 1.0)
                spread = []
                if scatter_z:
                    for k in range(1, pairs):
                        rows = fresh.at[:, place, :]
                        spread.append(Copy(rows, rows, (lax.rem(z + k, pairs) * 2 + core, t)))
                        spread[-1].start()
                    for copy in spread:
                        copy.arrived()
                rows = fresh.at[:, pl.ds(pl.multiple_of(start_row, tile_rows), tile_rows), :]
                gathers = []
                for k in range(1, tiles):
                    gathers.append(Copy(rows, rows, (s, lax.rem(t + k, tiles))))
                    gathers[-1].start()
                for copy in gathers:
                    copy.arrived()
                rows = fresh.at[:, pl.ds(pl.multiple_of(core * half_rows, half_rows), half_rows), :]
                swap = Copy(rows, rows, (s + 1 - 2 * core, t))
                swap.start()
                swap.arrived()
                for copy in [pair] + over_tiles + over_z + spread + gathers + [swap]:
                    copy.sent()

            for copy in halo:
                copy.arrived()
            for copy in halo + [up, down] + middle + upper + lower:
                copy.sent()

    probe_out[...] = probes[OUTER]


def per_device(stripes, tiles, positions, row_offsets, amplitudes, object_field, probe_field):
    patterns, size = amplitudes.shape[1], probe_field.shape[-1]
    own_rows, own_columns = object_field.shape[1:]
    forward, inverse = dft_blocks(size)
    passes = INNER * OUTER
    pairs = stripes // 2
    half_rows = size // 2
    tile_rows = half_rows // tiles
    z_rows = tile_rows // pairs
    if not (z_rows >= 8 and z_rows * pairs == tile_rows):
        z_rows = tile_rows
    count = 4 + passes * 10 + OUTER * (2 + 2 * (tiles - 1) + 2 * (pairs - 1))
    f32, bf16 = jnp.float32, jnp.bfloat16
    vmem = pl.BlockSpec(memory_space=pltpu.VMEM)
    return pl.pallas_call(
        functools.partial(kernel, stripes, tiles, patterns),
        out_shape=(
            jax.ShapeDtypeStruct(object_field.shape, f32),
            jax.ShapeDtypeStruct(probe_field.shape, f32),
        ),
        in_specs=[pl.BlockSpec(memory_space=pltpu.SMEM)] + [vmem] * 5,
        out_specs=(vmem, vmem),
        scratch_shapes=[
            pltpu.VMEM((2, own_rows + 2 * HALO , size), f32),
            pltpu.VMEM((2, own_rows + 2 * HALO, size), f32),
            pltpu.VMEM((2, size + 4 * HALO , size), f32),
            pltpu.VMEM((2, size, size), f32),
            pltpu.VMEM((2 * size, size), bf16),
            pltpu.VMEM((2 * size, size), bf16),
            pltpu.VMEM((passes + 1, 2, 2, own_rows, size // 2), f32),
            pltpu.VMEM((passes, 2, 2, HALO, size), f32),
            pltpu.VMEM((3, size, size), f32),
            pltpu.VMEM((OUTER + 1, 2, size, size), f32),
            pltpu.VMEM((OUTER, 3, half_rows, size), f32),
            pltpu.VMEM((3, half_rows, size), f32),
            pltpu.VMEM((OUTER, tiles - 1, 3, tile_rows, size), f32),
            pltpu.VMEM((3, tile_rows, size), f32),
            pltpu.VMEM((OUTER, pairs - 1, 3, z_rows, size), f32),
            pltpu.SemaphoreType.DMA((count,)),
            pltpu.SemaphoreType.DMA((count,)),
        ],
        compiler_params=pltpu.CompilerParams(
            collective_id=0, has_side_effects=True, vmem_limit_bytes=40 * 1024 * 1024
        ),
        name="refine",
    )(row_offsets, amplitudes, object_field, probe_field, jnp.asarray(forward), jnp.asarray(inverse))


def solution(mesh):
    placed = (
        P("stripe", "tile"),
        P("stripe", "tile"),
        P("stripe", "tile", None, None),
        P(None, "stripe", "tile"),
        P(),
    )
    return jax.shard_map(
        functools.partial(per_device, mesh.shape["stripe"], mesh.shape["tile"]),
        mesh=mesh,
        in_specs=placed,
        out_specs=(P(None, "stripe", "tile"), P()),
        check_vma=False,
    )
```

```python
import functools
import math

import jax
import jax.numpy as jnp
import ml_dtypes
import numpy as np
from jax import lax
from jax.experimental import pallas as pl
from jax.experimental.pallas import tpu as pltpu
from jax.sharding import PartitionSpec as P

HALO = 64
INNER = 2
OUTER = 2
CHUNK = 128
SUB = 8


def dft_blocks(size):
    indices = np.arange(size)
    angles = (indices[:, None] * indices[None, :] % size).astype(np.float64) * (2.0 * math.pi / size)
    factor = np.float32(1.0 / math.sqrt(size))
    cosine = (np.cos(angles).astype(np.float32) * factor).astype(ml_dtypes.bfloat16)
    sine = (np.sin(angles).astype(np.float32) * factor).astype(ml_dtypes.bfloat16)
    forward = np.block([[cosine, sine], [-sine, cosine]])
    inverse = np.block([[cosine, -sine], [sine, cosine]])
    return forward, inverse


def dot(a, b):
    return jnp.dot(a, b, preferred_element_type=jnp.float32)


def kernel(
    stripes, tiles, patterns,
    rows_ref, amp_hbm, obj_hbm, probe_hbm, fwd_hbm, inv_hbm,
    obj_out, probe_out,
    amp_ref, obj_ref, fwd_ref, inv_ref, packed, packs,
    ext, grad, shifted, window, exits, misses, cols, edges, totals, probes,
    pair_in, pair_sum, tile_in, tile_sum, z_in, load_sem, send_sem, recv_sem,
):
    size = probes.shape[-1]
    own_rows = obj_ref.shape[1]
    s = lax.axis_index("stripe")
    t = lax.axis_index("tile")
    core = lax.rem(s, 2)
    z = s // 2
    pairs = stripes // 2
    lo, hi = HALO, HALO + own_rows
    half_w = size // 2
    used = [0]

    class Copy:
        def __init__(self, src, dst, device, sends=None, receives=None):
            n = used[0]
            used[0] += 1
            self.sends, self.receives = sends, receives
            self.make = lambda: pltpu.make_async_remote_copy(
                src_ref=src, dst_ref=dst, send_sem=send_sem.at[n], recv_sem=recv_sem.at[n],
                device_id=device, device_id_type=pl.DeviceIdType.MESH,
            )

        def start(self):
            self.guard(self.sends, lambda: self.make().start())

        def sent(self):
            self.guard(self.sends, lambda: self.make().wait_send())

        def arrived(self):
            self.guard(self.receives, lambda: self.make().wait_recv())

        def guard(self, condition, act):
            if condition is None:
                act()
            else:
                pl.when(condition)(act)

    left, right = jnp.maximum(t - 1, 0), jnp.minimum(t + 1, tiles - 1)
    above, below = jnp.maximum(s - 1, 0), jnp.minimum(s + 1, stripes - 1)
    has_left, has_right = t > 0, t < tiles - 1
    has_above, has_below = s > 0, s < stripes - 1

    def to_left(src, dst):
        return Copy(src, dst, (s, left), has_left, has_right)

    def to_right(src, dst):
        return Copy(src, dst, (s, right), has_right, has_left)

    def to_above(src, dst):
        return Copy(src, dst, (above, t), has_above, has_below)

    def to_below(src, dst):
        return Copy(src, dst, (below, t), has_below, has_above)

    class Columns:
        def __init__(self, step, first, last):
            self.step, self.first, self.last = step, first, last
            rows = slice(lo + first, lo + last)
            self.copies = [
                to_left(grad.at[:, rows, :half_w], cols.at[step, 1, :, first:last, :]),
                to_right(grad.at[:, rows, half_w:], cols.at[step, 0, :, first:last, :]),
            ]
            for copy in self.copies:
                copy.start()

        def receive(self, scale):
            rows = slice(lo + self.first, lo + self.last)
            for copy in self.copies:
                copy.arrived()

            @pl.when(has_left)
            def _():
                ext[:, rows, :half_w] -= scale * cols[self.step, 0, :, self.first : self.last, :]

            @pl.when(has_right)
            def _():
                ext[:, rows, half_w:] -= scale * cols[self.step, 1, :, self.first : self.last, :]

    def packed_copies(n, first, last):
        copies = [
            to_left(packed.at[n, 0, first:last, :], packs.at[n, 1, first:last, :]),
            to_right(packed.at[n, 1, first:last, :], packs.at[n, 0, first:last, :]),
        ]
        for copy in copies:
            copy.start()
        return copies

    def turn(block):
        return pltpu.roll(block, HALO, 1)

    loads = [
        pltpu.make_async_copy(source, target, load_sem.at[n])
        for n, (source, target) in enumerate(
            [
                (obj_hbm, obj_ref),
                (probe_hbm, probes.at[0]),
                (fwd_hbm, fwd_ref),
                (inv_hbm, inv_ref),
                (amp_hbm, amp_ref),
            ]
        )
    ]
    for load in loads:
        load.start()
    lane = lax.broadcasted_iota(jnp.int32, (own_rows, half_w), 1)
    low = lane < HALO
    ext[:, :lo, :] = jnp.zeros((2, lo, size), jnp.float32)
    ext[:, hi:, :] = jnp.zeros((2, ext.shape[1] - hi, size), jnp.float32)

    barrier = pltpu.get_barrier_semaphore()

    def greet(device):
        pl.semaphore_signal(barrier, inc=1, device_id=device, device_id_type=pl.DeviceIdType.MESH)

    for k in range(1, tiles):
        greet((s, lax.rem(t + k, tiles)))
    for k in range(1, pairs):
        greet((lax.rem(z + k, pairs) * 2 + core, t))
    pl.when(has_above)(lambda: greet((above, t)))
    pl.when(has_below)(lambda: greet((below, t)))
    pl.semaphore_wait(
        barrier,
        tiles - 1 + pairs - 1 + has_above.astype(jnp.int32) + has_below.astype(jnp.int32),
    )

    loads[0].wait()
    packed[0, 0] = jnp.where(low, obj_ref[0], turn(obj_ref[1]))
    packed[0, 1] = jnp.where(low, turn(obj_ref[0]), obj_ref[1])
    first = [
        packed_copies(0, 0, HALO),
        packed_copies(0, own_rows - HALO, own_rows),
        packed_copies(0, HALO, own_rows - HALO),
    ]
    for part in range(2):
        turned = turn(obj_ref[part])
        ext[part, lo:hi, :half_w] = jnp.where(low, 0.0, turned)
        ext[part, lo:hi, half_w:] = jnp.where(low, turned, 0.0)

    def place_columns(copies, begin, end):
        rows = slice(lo + begin, lo + end)
        near = low[begin:end]
        for copy in copies:
            copy.arrived()

        @pl.when(has_left)
        def _():
            block = packs[0, 0, begin:end, :]
            ext[0, rows, :half_w] = jnp.where(near, block, ext[0, rows, :half_w])
            ext[1, rows, :half_w] = jnp.where(near, turn(block), ext[1, rows, :half_w])

        @pl.when(has_right)
        def _():
            block = packs[0, 1, begin:end, :]
            ext[0, rows, half_w:] = jnp.where(near, ext[0, rows, half_w:], turn(block))
            ext[1, rows, half_w:] = jnp.where(near, ext[1, rows, half_w:], block)

    def halo_above():
        copy = to_above(ext.at[:, lo : lo + HALO, :], ext.at[:, hi : hi + HALO, :])
        copy.start()
        return copy

    def halo_below():
        copy = to_below(ext.at[:, hi - HALO : hi, :], ext.at[:, :lo, :])
        copy.start()
        return copy

    place_columns(first[0], 0, HALO)
    halo = [halo_above()]
    place_columns(first[1], own_rows - HALO, own_rows)
    halo.append(halo_below())
    place_columns(first[2], HALO, own_rows - HALO)
    for load in loads[1:]:
        load.wait()
    for copy in halo:
        copy.arrived()
    for copy in halo + sum(first, []):
        copy.sent()

    offset = rows_ref[0, patterns - 1] + HALO

    top_bit = (2 * HALO).bit_length() - 1
    whole = offset == 2 * HALO

    def is_set(bit):
        return ((offset >> bit) & 1) == 1

    def rows_out():
        for part in range(2):
            for c in range(0, size, half_w):
                block = ext[part, :, c : c + half_w]
                for bit in reversed(range(top_bit)):
                    jump = 1 << bit
                    if jump >= SUB:
                        keep = block.shape[0] - jump
                        block = jnp.where(is_set(bit), block[jump:], block[:keep])
                    else:
                        turned = pltpu.roll(block, block.shape[0] - jump, 0)
                        block = jnp.where(is_set(bit), turned, block)
                window[part, :, c : c + half_w] = jnp.where(
                    whole, ext[part, 2 * HALO : 2 * HALO + size, c : c + half_w], block[:size]
                )

    def rows_in():
        for part in range(2):
            for c in range(0, size, half_w):
                patch = shifted[part, :, c : c + half_w]

                def zeros(rows):
                    return jnp.zeros((rows, half_w), jnp.float32)

                block = jnp.concatenate([patch, zeros(SUB)], axis=0)
                for bit in range(top_bit):
                    jump = 1 << bit
                    if jump >= SUB:
                        block = jnp.where(
                            is_set(bit),
                            jnp.concatenate([zeros(jump), block], axis=0),
                            jnp.concatenate([block, zeros(jump)], axis=0),
                        )
                    else:
                        block = jnp.where(is_set(bit), pltpu.roll(block, jump, 0), block)
                grad[part, :, c : c + half_w] = jnp.where(
                    whole,
                    jnp.concatenate([zeros(2 * HALO), patch], axis=0),
                    block[: size + 2 * HALO],
                )

    def pattern_pass(index, source, top, probe, target, base, accumulate, totals_mode):
        for r in range(0, size, CHUNK):
            w_re = source[0, top + r : top + r + CHUNK, :]
            w_im = source[1, top + r : top + r + CHUNK, :]
            p_re = probe[0, r : r + CHUNK, :]
            p_im = probe[1, r : r + CHUNK, :]
            exits[r : r + CHUNK, :] = (p_re * w_re - p_im * w_im).astype(jnp.bfloat16)
            exits[size + r : size + r + CHUNK, :] = (p_re * w_im + p_im * w_re).astype(jnp.bfloat16)
        for r in range(0, size, CHUNK):
            h_re = dot(fwd_ref[r : r + CHUNK, :], exits[...]).astype(jnp.bfloat16)
            h_im = dot(fwd_ref[size + r : size + r + CHUNK, :], exits[...]).astype(jnp.bfloat16)
            spec = dot(jnp.concatenate([h_re, h_im], axis=1), inv_ref[...])
            s_re, s_im = spec[:, :size], spec[:, size:]
            power = jnp.maximum(s_re * s_re + s_im * s_im, 0.25)
            scaling = amp_ref[0, index, r : r + CHUNK, :] * lax.rsqrt(power)
            misses[r : r + CHUNK, :] = (s_re - scaling * s_re).astype(jnp.bfloat16)
            misses[size + r : size + r + CHUNK, :] = (s_im - scaling * s_im).astype(jnp.bfloat16)
        for r in range(0, size, CHUNK):
            h_re = dot(inv_ref[r : r + CHUNK, :], misses[...]).astype(jnp.bfloat16)
            h_im = dot(inv_ref[size + r : size + r + CHUNK, :], misses[...]).astype(jnp.bfloat16)
            back = dot(jnp.concatenate([h_re, h_im], axis=1), fwd_ref[...])
            b_re, b_im = back[:, :size], back[:, size:]
            p_re = probe[0, r : r + CHUNK, :]
            p_im = probe[1, r : r + CHUNK, :]
            g_re = p_re * b_re + p_im * b_im
            g_im = p_re * b_im - p_im * b_re
            where = slice(base + r, base + r + CHUNK)
            if accumulate:
                g_re = g_re + target[0, where, :]
                g_im = g_im + target[1, where, :]
            target[0, where, :] = g_re
            target[1, where, :] = g_im
            if totals_mode is not None:
                w_re = source[0, top + r : top + r + CHUNK, :]
                w_im = source[1, top + r : top + r + CHUNK, :]
                q_re = w_re * b_re + w_im * b_im
                q_im = w_re * b_im - w_im * b_re
                light = w_re * w_re + w_im * w_im
                if totals_mode:
                    q_re = q_re + totals[0, r : r + CHUNK, :]
                    q_im = q_im + totals[1, r : r + CHUNK, :]
                    light = light + totals[2, r : r + CHUNK, :]
                totals[0, r : r + CHUNK, :] = q_re
                totals[1, r : r + CHUNK, :] = q_im
                totals[2, r : r + CHUNK, :] = light

    half_rows = size // 2
    tile_rows = half_rows // tiles
    z_rows = tile_rows // pairs
    scatter_z = z_rows >= 8 and z_rows * pairs == tile_rows

    for outer in range(OUTER):
        probe = probes.at[outer]
        fresh = probes.at[outer + 1]
        p_re, p_im = probe[0], probe[1]
        step_size = 1.0 / (2.0 * patterns * jnp.max(p_re * p_re + p_im * p_im) + 1e-06)
        for inner in range(INNER):
            step = outer * INNER + inner
            last_inner = inner == INNER - 1
            final = last_inner and outer == OUTER - 1
            rows_out()
            mode = (lambda later: later) if last_inner else (lambda later: None)
            pattern_pass(patterns - 1, window, 0, probe, shifted, 0, False, mode(False))
            rows_in()
            pattern_pass(0, ext, 0, probe, grad, 0, True, mode(True))
            up = to_above(grad.at[:, :lo, :], edges.at[step, 1])
            up.start()
            pattern_pass(1, ext, 2 * HALO, probe, grad, 2 * HALO, True, mode(True))
            down = to_below(grad.at[:, hi:, :], edges.at[step, 0])
            down.start()
            if last_inner:
                pair = Copy(
                    totals.at[:, pl.ds(pl.multiple_of((1 - core) * half_rows, half_rows), half_rows), :],
                    pair_in.at[outer],
                    (s + 1 - 2 * core, t),
                )
                pair.start()
            pieces = []
            up.arrived()

            @pl.when(has_below)
            def _():
                grad[:, hi - HALO : hi, :] += edges[step, 1]

            if not final:
                pieces.append(Columns(step, own_rows - HALO, own_rows))
            if last_inner:
                pair.arrived()
                kept = pl.ds(pl.multiple_of(core * half_rows, half_rows), half_rows)
                pair_sum[...] = totals[:, kept, :] + pair_in[outer]
                over_tiles = []
                for k in range(1, tiles):
                    to = lax.rem(t + k, tiles)
                    over_tiles.append(
                        Copy(
                            pair_sum.at[:, pl.ds(pl.multiple_of(to * tile_rows, tile_rows), tile_rows), :],
                            tile_in.at[outer, k - 1],
                            (s, to),
                        )
                    )
                    over_tiles[-1].start()
            if not final:
                pieces.append(Columns(step, HALO, own_rows // 2))
            down.arrived()

            @pl.when(has_above)
            def _():
                grad[:, lo : lo + HALO, :] += edges[step, 0]

            if not final:
                pieces.append(Columns(step, 0, HALO))
                pieces.append(Columns(step, own_rows // 2, own_rows - HALO))
            else:
                packed[1, 0] = jnp.where(low, grad[0, lo:hi, :half_w], turn(grad[1, lo:hi, :half_w]))
                packed[1, 1] = jnp.where(low, turn(grad[0, lo:hi, half_w:]), grad[1, lo:hi, half_w:])
                last = packed_copies(1, 0, own_rows)

            outside_left = jnp.logical_and(jnp.logical_not(has_left), low)
            outside_right = jnp.logical_and(jnp.logical_not(has_right), jnp.logical_not(low))
            for part in range(2):
                ext[part, lo:hi, :half_w] -= jnp.where(
                    outside_left, 0.0, step_size * grad[part, lo:hi, :half_w]
                )
                ext[part, lo:hi, half_w:] -= jnp.where(
                    outside_right, 0.0, step_size * grad[part, lo:hi, half_w:]
                )
            halo = []
            if not final:
                pieces[0].receive(step_size)
                halo.append(halo_below())
                pieces[2].receive(step_size)
                halo.append(halo_above())
            else:
                for part in range(2):
                    obj_out[part] = jnp.where(
                        low, turn(ext[part, lo:hi, :half_w]), turn(ext[part, lo:hi, half_w:])
                    )

            if last_inner:
                for copy in over_tiles:
                    copy.arrived()
                mine = pl.ds(pl.multiple_of(t * tile_rows, tile_rows), tile_rows)
                total = pair_sum[:, mine, :]
                for k in range(tiles - 1):
                    total = total + tile_in[outer, k]
                tile_sum[...] = total
                over_z = []
                for k in range(1, pairs):
                    to = lax.rem(z + k, pairs)
                    if scatter_z:
                        piece = pl.ds(pl.multiple_of(to * z_rows, z_rows), z_rows)
                        source = tile_sum.at[:, piece, :]
                    else:
                        source = tile_sum
                    over_z.append(Copy(source, z_in.at[outer, k - 1], (to * 2 + core, t)))
                    over_z[-1].start()
                if not final:
                    pieces[1].receive(step_size)
                    pieces[3].receive(step_size)
                for copy in over_z:
                    copy.arrived()
                start_row = core * half_rows + t * tile_rows
                if scatter_z:
                    total = tile_sum[:, pl.ds(pl.multiple_of(z * z_rows, z_rows), z_rows), :]
                    count = z_rows
                    new_row = start_row + z * z_rows
                else:
                    total = tile_sum[...]
                    count = tile_rows
                    new_row = start_row
                for k in range(pairs - 1):
                    total = total + z_in[outer, k]
                place = pl.ds(pl.multiple_of(new_row, count), count)
                fresh[:, place, :] = probe[:, place, :] - 0.5 * total[:2] / (total[2:] + 1.0)
                spread = []
                if scatter_z:
                    for k in range(1, pairs):
                        rows = fresh.at[:, place, :]
                        spread.append(Copy(rows, rows, (lax.rem(z + k, pairs) * 2 + core, t)))
                        spread[-1].start()
                    for copy in spread:
                        copy.arrived()
                rows = fresh.at[:, pl.ds(pl.multiple_of(start_row, tile_rows), tile_rows), :]
                gathers = []
                for k in range(1, tiles):
                    gathers.append(Copy(rows, rows, (s, lax.rem(t + k, tiles))))
                    gathers[-1].start()
                for copy in gathers:
                    copy.arrived()
                rows = fresh.at[:, pl.ds(pl.multiple_of(core * half_rows, half_rows), half_rows), :]
                swap = Copy(rows, rows, (s + 1 - 2 * core, t))
                swap.start()
                swap.arrived()
                for copy in [pair] + over_tiles + over_z + spread + gathers + [swap]:
                    copy.sent()

            if not last_inner:
                pieces[1].receive(step_size)
                pieces[3].receive(step_size)
            if final:
                for copy in last:
                    copy.arrived()

                @pl.when(has_left)
                def _():
                    block = step_size * packs[1, 0]
                    obj_out[0] -= jnp.where(low, block, 0.0)
                    obj_out[1] -= jnp.where(low, turn(block), 0.0)

                @pl.when(has_right)
                def _():
                    block = step_size * packs[1, 1]
                    obj_out[0] -= jnp.where(low, 0.0, turn(block))
                    obj_out[1] -= jnp.where(low, 0.0, block)

                for copy in last:
                    copy.sent()
            for copy in halo:
                copy.arrived()
            for copy in halo + [up, down] + sum([piece.copies for piece in pieces], []):
                copy.sent()

    probe_out[...] = probes[OUTER]


def per_device(stripes, tiles, positions, row_offsets, amplitudes, object_field, probe_field):
    patterns, size = amplitudes.shape[1], probe_field.shape[-1]
    own_rows, own_columns = object_field.shape[1:]
    forward, inverse = dft_blocks(size)
    passes = INNER * OUTER
    pairs = stripes // 2
    half_rows = size // 2
    tile_rows = half_rows // tiles
    z_rows = tile_rows // pairs
    if not (z_rows >= 8 and z_rows * pairs == tile_rows):
        z_rows = tile_rows
    count = 8 + (passes - 1) * 12 + 4 + OUTER * (2 + 2 * (tiles - 1) + 2 * (pairs - 1))
    f32, bf16 = jnp.float32, jnp.bfloat16
    vmem = pl.BlockSpec(memory_space=pltpu.VMEM)
    return pl.pallas_call(
        functools.partial(kernel, stripes, tiles, patterns),
        out_shape=(
            jax.ShapeDtypeStruct(object_field.shape, f32),
            jax.ShapeDtypeStruct(probe_field.shape, f32),
        ),
        in_specs=[pl.BlockSpec(memory_space=pltpu.SMEM)] + [pl.BlockSpec(memory_space=pltpu.HBM)] * 5,
        out_specs=(vmem, vmem),
        scratch_shapes=[
            pltpu.VMEM(amplitudes.shape, f32),
            pltpu.VMEM(object_field.shape, f32),
            pltpu.VMEM(forward.shape, bf16),
            pltpu.VMEM(inverse.shape, bf16),
            pltpu.VMEM((2, 2, own_rows, own_columns), f32),
            pltpu.VMEM((2, 2, own_rows, own_columns), f32),
            pltpu.VMEM((2, own_rows + 2 * HALO, size), f32),
            pltpu.VMEM((2, own_rows + 2 * HALO, size), f32),
            pltpu.VMEM((2, size, size), f32),
            pltpu.VMEM((2, size, size), f32),
            pltpu.VMEM((2 * size, size), bf16),
            pltpu.VMEM((2 * size, size), bf16),
            pltpu.VMEM((passes - 1, 2, 2, own_rows, size // 2), f32),
            pltpu.VMEM((passes, 2, 2, HALO, size), f32),
            pltpu.VMEM((3, size, size), f32),
            pltpu.VMEM((OUTER + 1, 2, size, size), f32),
            pltpu.VMEM((OUTER, 3, half_rows, size), f32),
            pltpu.VMEM((3, half_rows, size), f32),
            pltpu.VMEM((OUTER, tiles - 1, 3, tile_rows, size), f32),
            pltpu.VMEM((3, tile_rows, size), f32),
            pltpu.VMEM((OUTER, pairs - 1, 3, z_rows, size), f32),
            pltpu.SemaphoreType.DMA((5,)),
            pltpu.SemaphoreType.DMA((count,)),
            pltpu.SemaphoreType.DMA((count,)),
        ],
        compiler_params=pltpu.CompilerParams(
            collective_id=0, has_side_effects=True, vmem_limit_bytes=40 * 1024 * 1024
        ),
        name="refine",
    )(row_offsets, amplitudes, object_field, probe_field, jnp.asarray(forward), jnp.asarray(inverse))


def solution(mesh):
    placed = (
        P("stripe", "tile"),
        P("stripe", "tile"),
        P("stripe", "tile", None, None),
        P(None, "stripe", "tile"),
        P(),
    )
    return jax.shard_map(
        functools.partial(per_device, mesh.shape["stripe"], mesh.shape["tile"]),
        mesh=mesh,
        in_specs=placed,
        out_specs=(P(None, "stripe", "tile"), P()),
        check_vma=False,
    )
```

```python
import functools
import math

import jax
import jax.numpy as jnp
import ml_dtypes
import numpy as np
from jax import lax
from jax.experimental import pallas as pl
from jax.experimental.pallas import tpu as pltpu
from jax.sharding import PartitionSpec as P

HALO = 64
INNER = 2
OUTER = 2
CHUNK = 256
SUB = 8


def dft_blocks(size):
    indices = np.arange(size)
    angles = (indices[:, None] * indices[None, :] % size).astype(np.float64) * (2.0 * math.pi / size)
    factor = np.float32(1.0 / math.sqrt(size))
    cosine = (np.cos(angles).astype(np.float32) * factor).astype(ml_dtypes.bfloat16)
    sine = (np.sin(angles).astype(np.float32) * factor).astype(ml_dtypes.bfloat16)
    forward = np.block([[cosine, sine], [-sine, cosine]])
    inverse = np.block([[cosine, -sine], [sine, cosine]])
    return forward, inverse


def dot(a, b):
    return jnp.dot(a, b, preferred_element_type=jnp.float32)


def kernel(
    stripes, tiles, patterns,
    rows_ref, amp_hbm, obj_hbm, probe_hbm, fwd_hbm, inv_hbm,
    obj_out, probe_out,
    amp_ref, obj_ref, fwd_ref, inv_ref, packed, packs,
    ext, grad, shifted, window, exits, misses, cols, edges, totals, probes,
    pair_in, pair_sum, tile_in, tile_sum, z_in, load_sem, send_sem, recv_sem,
):
    size = probes.shape[-1]
    own_rows = obj_ref.shape[1]
    s = lax.axis_index("stripe")
    t = lax.axis_index("tile")
    core = lax.rem(s, 2)
    z = s // 2
    pairs = stripes // 2
    lo, hi = HALO, HALO + own_rows
    half_w = size // 2
    used = [0]

    class Copy:
        def __init__(self, src, dst, device, sends=None, receives=None):
            n = used[0]
            used[0] += 1
            self.sends, self.receives = sends, receives
            self.make = lambda: pltpu.make_async_remote_copy(
                src_ref=src, dst_ref=dst, send_sem=send_sem.at[n], recv_sem=recv_sem.at[n],
                device_id=device, device_id_type=pl.DeviceIdType.MESH,
            )

        def start(self):
            self.guard(self.sends, lambda: self.make().start())

        def sent(self):
            self.guard(self.sends, lambda: self.make().wait_send())

        def arrived(self):
            self.guard(self.receives, lambda: self.make().wait_recv())

        def guard(self, condition, act):
            if condition is None:
                act()
            else:
                pl.when(condition)(act)

    left, right = jnp.maximum(t - 1, 0), jnp.minimum(t + 1, tiles - 1)
    above, below = jnp.maximum(s - 1, 0), jnp.minimum(s + 1, stripes - 1)
    has_left, has_right = t > 0, t < tiles - 1
    has_above, has_below = s > 0, s < stripes - 1

    def to_left(src, dst):
        return Copy(src, dst, (s, left), has_left, has_right)

    def to_right(src, dst):
        return Copy(src, dst, (s, right), has_right, has_left)

    def to_above(src, dst):
        return Copy(src, dst, (above, t), has_above, has_below)

    def to_below(src, dst):
        return Copy(src, dst, (below, t), has_below, has_above)

    class Columns:
        def __init__(self, step, first, last):
            self.step, self.first, self.last = step, first, last
            rows = slice(lo + first, lo + last)
            self.copies = [
                to_left(grad.at[:, rows, :half_w], cols.at[step, 1, :, first:last, :]),
                to_right(grad.at[:, rows, half_w:], cols.at[step, 0, :, first:last, :]),
            ]
            for copy in self.copies:
                copy.start()

        def receive(self, scale):
            rows = slice(lo + self.first, lo + self.last)
            for copy in self.copies:
                copy.arrived()

            @pl.when(has_left)
            def _():
                ext[:, rows, :half_w] -= scale * cols[self.step, 0, :, self.first : self.last, :]

            @pl.when(has_right)
            def _():
                ext[:, rows, half_w:] -= scale * cols[self.step, 1, :, self.first : self.last, :]

    def packed_copies(n, first, last):
        copies = [
            to_left(packed.at[n, 0, first:last, :], packs.at[n, 1, first:last, :]),
            to_right(packed.at[n, 1, first:last, :], packs.at[n, 0, first:last, :]),
        ]
        for copy in copies:
            copy.start()
        return copies

    def turn(block):
        return pltpu.roll(block, HALO, 1)

    loads = [
        pltpu.make_async_copy(source, target, load_sem.at[n])
        for n, (source, target) in enumerate(
            [
                (obj_hbm, obj_ref),
                (probe_hbm, probes.at[0]),
                (fwd_hbm, fwd_ref),
                (inv_hbm, inv_ref),
                (amp_hbm, amp_ref),
            ]
        )
    ]
    for load in loads:
        load.start()
    lane = lax.broadcasted_iota(jnp.int32, (own_rows, half_w), 1)
    low = lane < HALO
    ext[:, :lo, :] = jnp.zeros((2, lo, size), jnp.float32)
    ext[:, hi:, :] = jnp.zeros((2, ext.shape[1] - hi, size), jnp.float32)

    barrier = pltpu.get_barrier_semaphore()

    def greet(device):
        pl.semaphore_signal(barrier, inc=1, device_id=device, device_id_type=pl.DeviceIdType.MESH)

    for k in range(1, tiles):
        greet((s, lax.rem(t + k, tiles)))
    for k in range(1, pairs):
        greet((lax.rem(z + k, pairs) * 2 + core, t))
    pl.when(has_above)(lambda: greet((above, t)))
    pl.when(has_below)(lambda: greet((below, t)))
    pl.semaphore_wait(
        barrier,
        tiles - 1 + pairs - 1 + has_above.astype(jnp.int32) + has_below.astype(jnp.int32),
    )

    loads[0].wait()
    packed[0, 0] = jnp.where(low, obj_ref[0], turn(obj_ref[1]))
    packed[0, 1] = jnp.where(low, turn(obj_ref[0]), obj_ref[1])
    first = [
        packed_copies(0, 0, HALO),
        packed_copies(0, own_rows - HALO, own_rows),
        packed_copies(0, HALO, own_rows - HALO),
    ]
    for part in range(2):
        turned = turn(obj_ref[part])
        ext[part, lo:hi, :half_w] = jnp.where(low, 0.0, turned)
        ext[part, lo:hi, half_w:] = jnp.where(low, turned, 0.0)

    def place_columns(copies, begin, end):
        rows = slice(lo + begin, lo + end)
        near = low[begin:end]
        for copy in copies:
            copy.arrived()

        @pl.when(has_left)
        def _():
            block = packs[0, 0, begin:end, :]
            ext[0, rows, :half_w] = jnp.where(near, block, ext[0, rows, :half_w])
            ext[1, rows, :half_w] = jnp.where(near, turn(block), ext[1, rows, :half_w])

        @pl.when(has_right)
        def _():
            block = packs[0, 1, begin:end, :]
            ext[0, rows, half_w:] = jnp.where(near, ext[0, rows, half_w:], turn(block))
            ext[1, rows, half_w:] = jnp.where(near, ext[1, rows, half_w:], block)

    def halo_above():
        copy = to_above(ext.at[:, lo : lo + HALO, :], ext.at[:, hi : hi + HALO, :])
        copy.start()
        return copy

    def halo_below():
        copy = to_below(ext.at[:, hi - HALO : hi, :], ext.at[:, :lo, :])
        copy.start()
        return copy

    place_columns(first[0], 0, HALO)
    halo = [halo_above()]
    place_columns(first[1], own_rows - HALO, own_rows)
    halo.append(halo_below())
    place_columns(first[2], HALO, own_rows - HALO)
    for load in loads[1:]:
        load.wait()
    for copy in halo:
        copy.arrived()
    for copy in halo + sum(first, []):
        copy.sent()

    offset = rows_ref[0, patterns - 1] + HALO

    top_bit = (2 * HALO).bit_length() - 1
    whole = offset == 2 * HALO

    def is_set(bit):
        return ((offset >> bit) & 1) == 1

    def rows_out():
        for part in range(2):
            for c in range(0, size, half_w):
                block = ext[part, :, c : c + half_w]
                for bit in reversed(range(top_bit)):
                    jump = 1 << bit
                    if jump >= SUB:
                        keep = block.shape[0] - jump
                        block = jnp.where(is_set(bit), block[jump:], block[:keep])
                    else:
                        turned = pltpu.roll(block, block.shape[0] - jump, 0)
                        block = jnp.where(is_set(bit), turned, block)
                window[part, :, c : c + half_w] = jnp.where(
                    whole, ext[part, 2 * HALO : 2 * HALO + size, c : c + half_w], block[:size]
                )

    def rows_in():
        for part in range(2):
            for c in range(0, size, half_w):
                patch = shifted[part, :, c : c + half_w]

                def zeros(rows):
                    return jnp.zeros((rows, half_w), jnp.float32)

                block = jnp.concatenate([patch, zeros(SUB)], axis=0)
                for bit in range(top_bit):
                    jump = 1 << bit
                    if jump >= SUB:
                        block = jnp.where(
                            is_set(bit),
                            jnp.concatenate([zeros(jump), block], axis=0),
                            jnp.concatenate([block, zeros(jump)], axis=0),
                        )
                    else:
                        block = jnp.where(is_set(bit), pltpu.roll(block, jump, 0), block)
                grad[part, :, c : c + half_w] = jnp.where(
                    whole,
                    jnp.concatenate([zeros(2 * HALO), patch], axis=0),
                    block[: size + 2 * HALO],
                )

    def pattern_pass(index, source, top, probe, target, base, accumulate, totals_mode):
        for r in range(0, size, CHUNK):
            w_re = source[0, top + r : top + r + CHUNK, :]
            w_im = source[1, top + r : top + r + CHUNK, :]
            p_re = probe[0, r : r + CHUNK, :]
            p_im = probe[1, r : r + CHUNK, :]
            exits[r : r + CHUNK, :] = (p_re * w_re - p_im * w_im).astype(jnp.bfloat16)
            exits[size + r : size + r + CHUNK, :] = (p_re * w_im + p_im * w_re).astype(jnp.bfloat16)
        half = dot(fwd_ref[...], exits[...]).astype(jnp.bfloat16)
        half = jnp.concatenate([half[:size], half[size:]], axis=1)
        for r in range(0, size, CHUNK):
            spec = dot(half[r : r + CHUNK], inv_ref[...])
            s_re, s_im = spec[:, :size], spec[:, size:]
            power = jnp.maximum(s_re * s_re + s_im * s_im, 0.25)
            scaling = amp_ref[0, index, r : r + CHUNK, :] * lax.rsqrt(power)
            misses[r : r + CHUNK, :] = (s_re - scaling * s_re).astype(jnp.bfloat16)
            misses[size + r : size + r + CHUNK, :] = (s_im - scaling * s_im).astype(jnp.bfloat16)
        half = dot(inv_ref[...], misses[...]).astype(jnp.bfloat16)
        half = jnp.concatenate([half[:size], half[size:]], axis=1)
        for r in range(0, size, CHUNK):
            back = dot(half[r : r + CHUNK], fwd_ref[...])
            b_re, b_im = back[:, :size], back[:, size:]
            p_re = probe[0, r : r + CHUNK, :]
            p_im = probe[1, r : r + CHUNK, :]
            g_re = p_re * b_re + p_im * b_im
            g_im = p_re * b_im - p_im * b_re
            where = slice(base + r, base + r + CHUNK)
            if accumulate:
                g_re = g_re + target[0, where, :]
                g_im = g_im + target[1, where, :]
            target[0, where, :] = g_re
            target[1, where, :] = g_im
            if totals_mode is not None:
                w_re = source[0, top + r : top + r + CHUNK, :]
                w_im = source[1, top + r : top + r + CHUNK, :]
                q_re = w_re * b_re + w_im * b_im
                q_im = w_re * b_im - w_im * b_re
                light = w_re * w_re + w_im * w_im
                if totals_mode:
                    q_re = q_re + totals[0, r : r + CHUNK, :]
                    q_im = q_im + totals[1, r : r + CHUNK, :]
                    light = light + totals[2, r : r + CHUNK, :]
                totals[0, r : r + CHUNK, :] = q_re
                totals[1, r : r + CHUNK, :] = q_im
                totals[2, r : r + CHUNK, :] = light

    half_rows = size // 2
    tile_rows = half_rows // tiles
    z_rows = tile_rows // pairs
    scatter_z = z_rows >= 8 and z_rows * pairs == tile_rows

    for outer in range(OUTER):
        probe = probes.at[outer]
        fresh = probes.at[outer + 1]
        p_re, p_im = probe[0], probe[1]
        step_size = 1.0 / (2.0 * patterns * jnp.max(p_re * p_re + p_im * p_im) + 1e-06)
        for inner in range(INNER):
            step = outer * INNER + inner
            last_inner = inner == INNER - 1
            final = last_inner and outer == OUTER - 1
            rows_out()
            mode = (lambda later: later) if last_inner else (lambda later: None)
            pattern_pass(patterns - 1, window, 0, probe, shifted, 0, False, mode(False))
            rows_in()
            pattern_pass(0, ext, 0, probe, grad, 0, True, mode(True))
            up = to_above(grad.at[:, :lo, :], edges.at[step, 1])
            up.start()
            pattern_pass(1, ext, 2 * HALO, probe, grad, 2 * HALO, True, mode(True))
            down = to_below(grad.at[:, hi:, :], edges.at[step, 0])
            down.start()
            if last_inner:
                pair = Copy(
                    totals.at[:, pl.ds(pl.multiple_of((1 - core) * half_rows, half_rows), half_rows), :],
                    pair_in.at[outer],
                    (s + 1 - 2 * core, t),
                )
                pair.start()
            pieces = []
            up.arrived()

            @pl.when(has_below)
            def _():
                grad[:, hi - HALO : hi, :] += edges[step, 1]

            if not final:
                pieces.append(Columns(step, own_rows - HALO, own_rows))
            if last_inner:
                pair.arrived()
                kept = pl.ds(pl.multiple_of(core * half_rows, half_rows), half_rows)
                pair_sum[...] = totals[:, kept, :] + pair_in[outer]
                over_tiles = []
                for k in range(1, tiles):
                    to = lax.rem(t + k, tiles)
                    over_tiles.append(
                        Copy(
                            pair_sum.at[:, pl.ds(pl.multiple_of(to * tile_rows, tile_rows), tile_rows), :],
                            tile_in.at[outer, k - 1],
                            (s, to),
                        )
                    )
                    over_tiles[-1].start()
            if not final:
                pieces.append(Columns(step, HALO, own_rows // 2))
            down.arrived()

            @pl.when(has_above)
            def _():
                grad[:, lo : lo + HALO, :] += edges[step, 0]

            if not final:
                pieces.append(Columns(step, 0, HALO))
                pieces.append(Columns(step, own_rows // 2, own_rows - HALO))
            else:
                packed[1, 0] = jnp.where(low, grad[0, lo:hi, :half_w], turn(grad[1, lo:hi, :half_w]))
                packed[1, 1] = jnp.where(low, turn(grad[0, lo:hi, half_w:]), grad[1, lo:hi, half_w:])
                last = packed_copies(1, 0, own_rows)

            outside_left = jnp.logical_and(jnp.logical_not(has_left), low)
            outside_right = jnp.logical_and(jnp.logical_not(has_right), jnp.logical_not(low))
            for part in range(2):
                ext[part, lo:hi, :half_w] -= jnp.where(
                    outside_left, 0.0, step_size * grad[part, lo:hi, :half_w]
                )
                ext[part, lo:hi, half_w:] -= jnp.where(
                    outside_right, 0.0, step_size * grad[part, lo:hi, half_w:]
                )
            halo = []
            if not final:
                pieces[0].receive(step_size)
                halo.append(halo_below())
                pieces[2].receive(step_size)
                halo.append(halo_above())
            else:
                for part in range(2):
                    obj_out[part] = jnp.where(
                        low, turn(ext[part, lo:hi, :half_w]), turn(ext[part, lo:hi, half_w:])
                    )

            if last_inner:
                for copy in over_tiles:
                    copy.arrived()
                mine = pl.ds(pl.multiple_of(t * tile_rows, tile_rows), tile_rows)
                total = pair_sum[:, mine, :]
                for k in range(tiles - 1):
                    total = total + tile_in[outer, k]
                tile_sum[...] = total
                over_z = []
                for k in range(1, pairs):
                    to = lax.rem(z + k, pairs)
                    if scatter_z:
                        piece = pl.ds(pl.multiple_of(to * z_rows, z_rows), z_rows)
                        source = tile_sum.at[:, piece, :]
                    else:
                        source = tile_sum
                    over_z.append(Copy(source, z_in.at[outer, k - 1], (to * 2 + core, t)))
                    over_z[-1].start()
                if not final:
                    pieces[1].receive(step_size)
                    pieces[3].receive(step_size)
                for copy in over_z:
                    copy.arrived()
                start_row = core * half_rows + t * tile_rows
                if scatter_z:
                    total = tile_sum[:, pl.ds(pl.multiple_of(z * z_rows, z_rows), z_rows), :]
                    count = z_rows
                    new_row = start_row + z * z_rows
                else:
                    total = tile_sum[...]
                    count = tile_rows
                    new_row = start_row
                for k in range(pairs - 1):
                    total = total + z_in[outer, k]
                place = pl.ds(pl.multiple_of(new_row, count), count)
                fresh[:, place, :] = probe[:, place, :] - 0.5 * total[:2] / (total[2:] + 1.0)
                spread = []
                if scatter_z:
                    for k in range(1, pairs):
                        rows = fresh.at[:, place, :]
                        spread.append(Copy(rows, rows, (lax.rem(z + k, pairs) * 2 + core, t)))
                        spread[-1].start()
                    for copy in spread:
                        copy.arrived()
                rows = fresh.at[:, pl.ds(pl.multiple_of(start_row, tile_rows), tile_rows), :]
                gathers = []
                for k in range(1, tiles):
                    gathers.append(Copy(rows, rows, (s, lax.rem(t + k, tiles))))
                    gathers[-1].start()
                for copy in gathers:
                    copy.arrived()
                rows = fresh.at[:, pl.ds(pl.multiple_of(core * half_rows, half_rows), half_rows), :]
                swap = Copy(rows, rows, (s + 1 - 2 * core, t))
                swap.start()
                swap.arrived()
                for copy in [pair] + over_tiles + over_z + spread + gathers + [swap]:
                    copy.sent()

            if not last_inner:
                pieces[1].receive(step_size)
                pieces[3].receive(step_size)
            if final:
                for copy in last:
                    copy.arrived()

                @pl.when(has_left)
                def _():
                    block = step_size * packs[1, 0]
                    obj_out[0] -= jnp.where(low, block, 0.0)
                    obj_out[1] -= jnp.where(low, turn(block), 0.0)

                @pl.when(has_right)
                def _():
                    block = step_size * packs[1, 1]
                    obj_out[0] -= jnp.where(low, 0.0, turn(block))
                    obj_out[1] -= jnp.where(low, 0.0, block)

                for copy in last:
                    copy.sent()
            for copy in halo:
                copy.arrived()
            for copy in halo + [up, down] + sum([piece.copies for piece in pieces], []):
                copy.sent()

    probe_out[...] = probes[OUTER]


def per_device(stripes, tiles, positions, row_offsets, amplitudes, object_field, probe_field):
    patterns, size = amplitudes.shape[1], probe_field.shape[-1]
    own_rows, own_columns = object_field.shape[1:]
    forward, inverse = dft_blocks(size)
    passes = INNER * OUTER
    pairs = stripes // 2
    half_rows = size // 2
    tile_rows = half_rows // tiles
    z_rows = tile_rows // pairs
    if not (z_rows >= 8 and z_rows * pairs == tile_rows):
        z_rows = tile_rows
    count = 8 + (passes - 1) * 12 + 4 + OUTER * (2 + 2 * (tiles - 1) + 2 * (pairs - 1))
    f32, bf16 = jnp.float32, jnp.bfloat16
    vmem = pl.BlockSpec(memory_space=pltpu.VMEM)
    return pl.pallas_call(
        functools.partial(kernel, stripes, tiles, patterns),
        out_shape=(
            jax.ShapeDtypeStruct(object_field.shape, f32),
            jax.ShapeDtypeStruct(probe_field.shape, f32),
        ),
        in_specs=[pl.BlockSpec(memory_space=pltpu.SMEM)] + [pl.BlockSpec(memory_space=pltpu.HBM)] * 5,
        out_specs=(vmem, vmem),
        scratch_shapes=[
            pltpu.VMEM(amplitudes.shape, f32),
            pltpu.VMEM(object_field.shape, f32),
            pltpu.VMEM(forward.shape, bf16),
            pltpu.VMEM(inverse.shape, bf16),
            pltpu.VMEM((2, 2, own_rows, own_columns), f32),
            pltpu.VMEM((2, 2, own_rows, own_columns), f32),
            pltpu.VMEM((2, own_rows + 2 * HALO, size), f32),
            pltpu.VMEM((2, own_rows + 2 * HALO, size), f32),
            pltpu.VMEM((2, size, size), f32),
            pltpu.VMEM((2, size, size), f32),
            pltpu.VMEM((2 * size, size), bf16),
            pltpu.VMEM((2 * size, size), bf16),
            pltpu.VMEM((passes - 1, 2, 2, own_rows, size // 2), f32),
            pltpu.VMEM((passes, 2, 2, HALO, size), f32),
            pltpu.VMEM((3, size, size), f32),
            pltpu.VMEM((OUTER + 1, 2, size, size), f32),
            pltpu.VMEM((OUTER, 3, half_rows, size), f32),
            pltpu.VMEM((3, half_rows, size), f32),
            pltpu.VMEM((OUTER, tiles - 1, 3, tile_rows, size), f32),
            pltpu.VMEM((3, tile_rows, size), f32),
            pltpu.VMEM((OUTER, pairs - 1, 3, z_rows, size), f32),
            pltpu.SemaphoreType.DMA((5,)),
            pltpu.SemaphoreType.DMA((count,)),
            pltpu.SemaphoreType.DMA((count,)),
        ],
        compiler_params=pltpu.CompilerParams(
            collective_id=0, has_side_effects=True, vmem_limit_bytes=64 * 1024 * 1024
        ),
        name="refine",
    )(row_offsets, amplitudes, object_field, probe_field, jnp.asarray(forward), jnp.asarray(inverse))


def solution(mesh):
    placed = (
        P("stripe", "tile"),
        P("stripe", "tile"),
        P("stripe", "tile", None, None),
        P(None, "stripe", "tile"),
        P(),
    )
    return jax.shard_map(
        functools.partial(per_device, mesh.shape["stripe"], mesh.shape["tile"]),
        mesh=mesh,
        in_specs=placed,
        out_specs=(P(None, "stripe", "tile"), P()),
        check_vma=False,
    )
```

```python
import functools
import math

import jax
import jax.numpy as jnp
import ml_dtypes
import numpy as np
from jax import lax
from jax.experimental import pallas as pl
from jax.experimental.pallas import tpu as pltpu
from jax.sharding import PartitionSpec as P

HALO = 64
INNER = 2
OUTER = 2
CHUNK = 256
SUB = 8


def dft_blocks(size):
    indices = np.arange(size)
    angles = (indices[:, None] * indices[None, :] % size).astype(np.float64) * (2.0 * math.pi / size)
    factor = np.float32(1.0 / math.sqrt(size))
    cosine = (np.cos(angles).astype(np.float32) * factor).astype(ml_dtypes.bfloat16)
    sine = (np.sin(angles).astype(np.float32) * factor).astype(ml_dtypes.bfloat16)
    forward = np.block([[cosine, sine], [-sine, cosine]])
    inverse = np.block([[cosine, -sine], [sine, cosine]])
    return forward, inverse


def dot(a, b):
    return jnp.dot(a, b, preferred_element_type=jnp.float32)


def kernel(
    stripes, tiles, patterns,
    rows_ref, amp_hbm, obj_hbm, probe_hbm, fwd_hbm, inv_hbm,
    obj_out, probe_out,
    amp_ref, obj_ref, fwd_ref, inv_ref, packed, packs,
    ext, grad, shifted, window, exits, misses, cols, edges, totals, probes,
    pair_in, pair_sum, tile_in, tile_sum, z_in, load_sem, send_sem, recv_sem,
):
    size = probes.shape[-1]
    own_rows = obj_ref.shape[1]
    s = lax.axis_index("stripe")
    t = lax.axis_index("tile")
    core = lax.rem(s, 2)
    z = s // 2
    pairs = stripes // 2
    lo, hi = HALO, HALO + own_rows
    half_w = size // 2
    used = [0]

    class Copy:
        def __init__(self, src, dst, device, sends=None, receives=None):
            n = used[0]
            used[0] += 1
            self.sends, self.receives = sends, receives
            self.make = lambda: pltpu.make_async_remote_copy(
                src_ref=src, dst_ref=dst, send_sem=send_sem.at[n], recv_sem=recv_sem.at[n],
                device_id=device, device_id_type=pl.DeviceIdType.MESH,
            )

        def start(self):
            self.guard(self.sends, lambda: self.make().start())

        def sent(self):
            self.guard(self.sends, lambda: self.make().wait_send())

        def arrived(self):
            self.guard(self.receives, lambda: self.make().wait_recv())

        def guard(self, condition, act):
            if condition is None:
                act()
            else:
                pl.when(condition)(act)

    left, right = jnp.maximum(t - 1, 0), jnp.minimum(t + 1, tiles - 1)
    above, below = jnp.maximum(s - 1, 0), jnp.minimum(s + 1, stripes - 1)
    has_left, has_right = t > 0, t < tiles - 1
    has_above, has_below = s > 0, s < stripes - 1

    def to_left(src, dst):
        return Copy(src, dst, (s, left), has_left, has_right)

    def to_right(src, dst):
        return Copy(src, dst, (s, right), has_right, has_left)

    def to_above(src, dst):
        return Copy(src, dst, (above, t), has_above, has_below)

    def to_below(src, dst):
        return Copy(src, dst, (below, t), has_below, has_above)

    class Columns:
        def __init__(self, step, first, last):
            self.step, self.first, self.last = step, first, last
            rows = slice(lo + first, lo + last)
            self.copies = [
                to_left(grad.at[:, rows, :half_w], cols.at[step, 1, :, first:last, :]),
                to_right(grad.at[:, rows, half_w:], cols.at[step, 0, :, first:last, :]),
            ]
            for copy in self.copies:
                copy.start()

        def receive(self, scale):
            rows = slice(lo + self.first, lo + self.last)
            for copy in self.copies:
                copy.arrived()

            @pl.when(has_left)
            def _():
                ext[:, rows, :half_w] -= scale * cols[self.step, 0, :, self.first : self.last, :]

            @pl.when(has_right)
            def _():
                ext[:, rows, half_w:] -= scale * cols[self.step, 1, :, self.first : self.last, :]

    def packed_copies(n, first, last):
        copies = [
            to_left(packed.at[n, 0, first:last, :], packs.at[n, 1, first:last, :]),
            to_right(packed.at[n, 1, first:last, :], packs.at[n, 0, first:last, :]),
        ]
        for copy in copies:
            copy.start()
        return copies

    def turn(block):
        return pltpu.roll(block, HALO, 1)

    loads = [
        pltpu.make_async_copy(source, target, load_sem.at[n])
        for n, (source, target) in enumerate(
            [
                (obj_hbm, obj_ref),
                (probe_hbm, probes.at[0]),
                (fwd_hbm, fwd_ref),
                (inv_hbm, inv_ref),
                (amp_hbm, amp_ref),
            ]
        )
    ]
    for load in loads:
        load.start()
    lane = lax.broadcasted_iota(jnp.int32, (own_rows, half_w), 1)
    low = lane < HALO
    ext[:, :lo, :] = jnp.zeros((2, lo, size), jnp.float32)
    ext[:, hi:, :] = jnp.zeros((2, ext.shape[1] - hi, size), jnp.float32)

    barrier = pltpu.get_barrier_semaphore()

    def greet(device):
        pl.semaphore_signal(barrier, inc=1, device_id=device, device_id_type=pl.DeviceIdType.MESH)

    for k in range(1, tiles):
        greet((s, lax.rem(t + k, tiles)))
    for k in range(1, pairs):
        greet((lax.rem(z + k, pairs) * 2 + core, t))
    pl.when(has_above)(lambda: greet((above, t)))
    pl.when(has_below)(lambda: greet((below, t)))
    pl.semaphore_wait(
        barrier,
        tiles - 1 + pairs - 1 + has_above.astype(jnp.int32) + has_below.astype(jnp.int32),
    )

    loads[0].wait()
    packed[0, 0] = jnp.where(low, obj_ref[0], turn(obj_ref[1]))
    packed[0, 1] = jnp.where(low, turn(obj_ref[0]), obj_ref[1])
    first = [
        packed_copies(0, 0, HALO),
        packed_copies(0, own_rows - HALO, own_rows),
        packed_copies(0, HALO, own_rows - HALO),
    ]
    for part in range(2):
        turned = turn(obj_ref[part])
        ext[part, lo:hi, :half_w] = jnp.where(low, 0.0, turned)
        ext[part, lo:hi, half_w:] = jnp.where(low, turned, 0.0)

    def place_columns(copies, begin, end):
        rows = slice(lo + begin, lo + end)
        near = low[begin:end]
        for copy in copies:
            copy.arrived()

        @pl.when(has_left)
        def _():
            block = packs[0, 0, begin:end, :]
            ext[0, rows, :half_w] = jnp.where(near, block, ext[0, rows, :half_w])
            ext[1, rows, :half_w] = jnp.where(near, turn(block), ext[1, rows, :half_w])

        @pl.when(has_right)
        def _():
            block = packs[0, 1, begin:end, :]
            ext[0, rows, half_w:] = jnp.where(near, ext[0, rows, half_w:], turn(block))
            ext[1, rows, half_w:] = jnp.where(near, ext[1, rows, half_w:], block)

    def halo_above():
        copy = to_above(ext.at[:, lo : lo + HALO, :], ext.at[:, hi : hi + HALO, :])
        copy.start()
        return copy

    def halo_below():
        copy = to_below(ext.at[:, hi - HALO : hi, :], ext.at[:, :lo, :])
        copy.start()
        return copy

    place_columns(first[0], 0, HALO)
    halo = [halo_above()]
    place_columns(first[1], own_rows - HALO, own_rows)
    halo.append(halo_below())
    place_columns(first[2], HALO, own_rows - HALO)
    for load in loads[1:]:
        load.wait()
    for copy in halo:
        copy.arrived()
    for copy in halo + sum(first, []):
        copy.sent()

    offset = rows_ref[0, patterns - 1] + HALO

    top_bit = (2 * HALO).bit_length() - 1
    whole = offset == 2 * HALO

    def is_set(bit):
        return ((offset >> bit) & 1) == 1

    def rows_out():
        for part in range(2):
            for c in range(0, size, half_w):
                block = ext[part, :, c : c + half_w]
                for bit in reversed(range(top_bit)):
                    jump = 1 << bit
                    if jump >= SUB:
                        keep = block.shape[0] - jump
                        block = jnp.where(is_set(bit), block[jump:], block[:keep])
                    else:
                        turned = pltpu.roll(block, block.shape[0] - jump, 0)
                        block = jnp.where(is_set(bit), turned, block)
                window[part, :, c : c + half_w] = jnp.where(
                    whole, ext[part, 2 * HALO : 2 * HALO + size, c : c + half_w], block[:size]
                )

    def rows_in():
        for part in range(2):
            for c in range(0, size, half_w):
                patch = shifted[part, :, c : c + half_w]

                def zeros(rows):
                    return jnp.zeros((rows, half_w), jnp.float32)

                block = jnp.concatenate([patch, zeros(SUB)], axis=0)
                for bit in range(top_bit):
                    jump = 1 << bit
                    if jump >= SUB:
                        block = jnp.where(
                            is_set(bit),
                            jnp.concatenate([zeros(jump), block], axis=0),
                            jnp.concatenate([block, zeros(jump)], axis=0),
                        )
                    else:
                        block = jnp.where(is_set(bit), pltpu.roll(block, jump, 0), block)
                grad[part, :, c : c + half_w] = jnp.where(
                    whole,
                    jnp.concatenate([zeros(2 * HALO), patch], axis=0),
                    block[: size + 2 * HALO],
                )

    def pattern_pass(index, source, top, probe, target, base, accumulate, totals_mode):
        for r in range(0, size, CHUNK):
            w_re = source[0, top + r : top + r + CHUNK, :]
            w_im = source[1, top + r : top + r + CHUNK, :]
            p_re = probe[0, r : r + CHUNK, :]
            p_im = probe[1, r : r + CHUNK, :]
            exits[r : r + CHUNK, :] = (p_re * w_re - p_im * w_im).astype(jnp.bfloat16)
            exits[size + r : size + r + CHUNK, :] = (p_re * w_im + p_im * w_re).astype(jnp.bfloat16)
        half = dot(fwd_ref[...], exits[...]).astype(jnp.bfloat16)
        half = jnp.concatenate([half[:size], half[size:]], axis=1)
        for r in range(0, size, CHUNK):
            spec = dot(half[r : r + CHUNK], inv_ref[...])
            s_re, s_im = spec[:, :size], spec[:, size:]
            power = jnp.maximum(s_re * s_re + s_im * s_im, 0.25)
            scaling = amp_ref[0, index, r : r + CHUNK, :] * lax.rsqrt(power)
            misses[r : r + CHUNK, :] = (s_re - scaling * s_re).astype(jnp.bfloat16)
            misses[size + r : size + r + CHUNK, :] = (s_im - scaling * s_im).astype(jnp.bfloat16)
        half = dot(inv_ref[...], misses[...]).astype(jnp.bfloat16)
        half = jnp.concatenate([half[:size], half[size:]], axis=1)
        for r in range(0, size, CHUNK):
            back = dot(half[r : r + CHUNK], fwd_ref[...])
            b_re, b_im = back[:, :size], back[:, size:]
            p_re = probe[0, r : r + CHUNK, :]
            p_im = probe[1, r : r + CHUNK, :]
            g_re = p_re * b_re + p_im * b_im
            g_im = p_re * b_im - p_im * b_re
            where = slice(base + r, base + r + CHUNK)
            if accumulate:
                g_re = g_re + target[0, where, :]
                g_im = g_im + target[1, where, :]
            target[0, where, :] = g_re
            target[1, where, :] = g_im
            if totals_mode is not None:
                w_re = source[0, top + r : top + r + CHUNK, :]
                w_im = source[1, top + r : top + r + CHUNK, :]
                q_re = w_re * b_re + w_im * b_im
                q_im = w_re * b_im - w_im * b_re
                if totals_mode:
                    q_re = q_re + totals[0, r : r + CHUNK, :]
                    q_im = q_im + totals[1, r : r + CHUNK, :]
                totals[0, r : r + CHUNK, :] = q_re
                totals[1, r : r + CHUNK, :] = q_im

    half_rows = size // 2
    tile_rows = half_rows // tiles
    z_rows = tile_rows // pairs
    scatter_z = z_rows >= 8 and z_rows * pairs == tile_rows

    kept = pl.ds(pl.multiple_of(core * half_rows, half_rows), half_rows)
    given = pl.ds(pl.multiple_of((1 - core) * half_rows, half_rows), half_rows)
    mine = pl.ds(pl.multiple_of(t * tile_rows, tile_rows), tile_rows)

    class Totals:
        def __init__(self, outer, parts):
            self.outer, self.parts = outer, parts
            self.pair = Copy(
                totals.at[parts, given, :], pair_in.at[outer, parts], (s + 1 - 2 * core, t)
            )
            self.pair.start()

        def to_tiles(self):
            self.pair.arrived()
            pair_sum[self.parts] = totals[self.parts, kept, :] + pair_in[self.outer, self.parts]
            self.over_tiles = []
            for k in range(1, tiles):
                to = lax.rem(t + k, tiles)
                there = pl.ds(pl.multiple_of(to * tile_rows, tile_rows), tile_rows)
                copy = Copy(
                    pair_sum.at[self.parts, there, :],
                    tile_in.at[self.outer, k - 1, self.parts],
                    (s, to),
                )
                copy.start()
                self.over_tiles.append(copy)

        def to_z(self):
            for copy in self.over_tiles:
                copy.arrived()
            total = pair_sum[self.parts, mine, :]
            for k in range(tiles - 1):
                total = total + tile_in[self.outer, k, self.parts]
            tile_sum[self.parts] = total
            self.over_z = []
            for k in range(1, pairs):
                to = lax.rem(z + k, pairs)
                if scatter_z:
                    there = pl.ds(pl.multiple_of(to * z_rows, z_rows), z_rows)
                    source = tile_sum.at[self.parts, there, :]
                else:
                    source = tile_sum.at[self.parts]
                copy = Copy(source, z_in.at[self.outer, k - 1, self.parts], (to * 2 + core, t))
                copy.start()
                self.over_z.append(copy)

        def arrived(self):
            for copy in self.over_z:
                copy.arrived()

        def sent(self):
            for copy in [self.pair] + self.over_tiles + self.over_z:
                copy.sent()

    for outer in range(OUTER):
        probe = probes.at[outer]
        fresh = probes.at[outer + 1]
        p_re, p_im = probe[0], probe[1]
        step_size = 1.0 / (2.0 * patterns * jnp.max(p_re * p_re + p_im * p_im) + 1e-06)
        for inner in range(INNER):
            step = outer * INNER + inner
            last_inner = inner == INNER - 1
            final = last_inner and outer == OUTER - 1
            rows_out()
            mode = (lambda later: later) if last_inner else (lambda later: None)
            if last_inner:
                for r in range(0, size, CHUNK):
                    light = 0.0
                    for source, top in ((window, 0), (ext, 0), (ext, 2 * HALO)):
                        w_re = source[0, top + r : top + r + CHUNK, :]
                        w_im = source[1, top + r : top + r + CHUNK, :]
                        light = light + (w_re * w_re + w_im * w_im)
                    totals[2, r : r + CHUNK, :] = light
                lights = Totals(outer, slice(2, 3))
            pattern_pass(patterns - 1, window, 0, probe, shifted, 0, False, mode(False))
            rows_in()
            if last_inner:
                lights.to_tiles()
            pattern_pass(0, ext, 0, probe, grad, 0, True, mode(True))
            up = to_above(grad.at[:, :lo, :], edges.at[step, 1])
            up.start()
            if last_inner:
                lights.to_z()
            pattern_pass(1, ext, 2 * HALO, probe, grad, 2 * HALO, True, mode(True))
            down = to_below(grad.at[:, hi:, :], edges.at[step, 0])
            down.start()
            if last_inner:
                slopes = Totals(outer, slice(0, 2))
            pieces = []
            up.arrived()

            @pl.when(has_below)
            def _():
                grad[:, hi - HALO : hi, :] += edges[step, 1]

            if not final:
                pieces.append(Columns(step, own_rows - HALO, own_rows))
            if last_inner:
                slopes.to_tiles()
            if not final:
                pieces.append(Columns(step, HALO, own_rows // 2))
            down.arrived()

            @pl.when(has_above)
            def _():
                grad[:, lo : lo + HALO, :] += edges[step, 0]

            if not final:
                pieces.append(Columns(step, 0, HALO))
                pieces.append(Columns(step, own_rows // 2, own_rows - HALO))
            else:
                packed[1, 0] = jnp.where(low, grad[0, lo:hi, :half_w], turn(grad[1, lo:hi, :half_w]))
                packed[1, 1] = jnp.where(low, turn(grad[0, lo:hi, half_w:]), grad[1, lo:hi, half_w:])
                last = packed_copies(1, 0, own_rows)

            outside_left = jnp.logical_and(jnp.logical_not(has_left), low)
            outside_right = jnp.logical_and(jnp.logical_not(has_right), jnp.logical_not(low))
            for part in range(2):
                ext[part, lo:hi, :half_w] -= jnp.where(
                    outside_left, 0.0, step_size * grad[part, lo:hi, :half_w]
                )
                ext[part, lo:hi, half_w:] -= jnp.where(
                    outside_right, 0.0, step_size * grad[part, lo:hi, half_w:]
                )
            halo = []
            if not final:
                pieces[0].receive(step_size)
                halo.append(halo_below())
                pieces[2].receive(step_size)
                halo.append(halo_above())
            else:
                for part in range(2):
                    obj_out[part] = jnp.where(
                        low, turn(ext[part, lo:hi, :half_w]), turn(ext[part, lo:hi, half_w:])
                    )

            if last_inner:
                slopes.to_z()
                if not final:
                    pieces[1].receive(step_size)
                    pieces[3].receive(step_size)
                slopes.arrived()
                lights.arrived()
                start_row = core * half_rows + t * tile_rows
                if scatter_z:
                    total = tile_sum[:, pl.ds(pl.multiple_of(z * z_rows, z_rows), z_rows), :]
                    count = z_rows
                    new_row = start_row + z * z_rows
                else:
                    total = tile_sum[...]
                    count = tile_rows
                    new_row = start_row
                for k in range(pairs - 1):
                    total = total + z_in[outer, k]
                place = pl.ds(pl.multiple_of(new_row, count), count)
                fresh[:, place, :] = probe[:, place, :] - 0.5 * total[:2] / (total[2:] + 1.0)
                spread = []
                if scatter_z:
                    for k in range(1, pairs):
                        rows = fresh.at[:, place, :]
                        spread.append(Copy(rows, rows, (lax.rem(z + k, pairs) * 2 + core, t)))
                        spread[-1].start()
                    for copy in spread:
                        copy.arrived()
                rows = fresh.at[:, pl.ds(pl.multiple_of(start_row, tile_rows), tile_rows), :]
                gathers = []
                for k in range(1, tiles):
                    gathers.append(Copy(rows, rows, (s, lax.rem(t + k, tiles))))
                    gathers[-1].start()
                for copy in gathers:
                    copy.arrived()
                rows = fresh.at[:, pl.ds(pl.multiple_of(core * half_rows, half_rows), half_rows), :]
                swap = Copy(rows, rows, (s + 1 - 2 * core, t))
                swap.start()
                swap.arrived()
                for copy in spread + gathers + [swap]:
                    copy.sent()
                slopes.sent()
                lights.sent()

            if not last_inner:
                pieces[1].receive(step_size)
                pieces[3].receive(step_size)
            if final:
                for copy in last:
                    copy.arrived()

                @pl.when(has_left)
                def _():
                    block = step_size * packs[1, 0]
                    obj_out[0] -= jnp.where(low, block, 0.0)
                    obj_out[1] -= jnp.where(low, turn(block), 0.0)

                @pl.when(has_right)
                def _():
                    block = step_size * packs[1, 1]
                    obj_out[0] -= jnp.where(low, 0.0, turn(block))
                    obj_out[1] -= jnp.where(low, 0.0, block)

                for copy in last:
                    copy.sent()
            for copy in halo:
                copy.arrived()
            for copy in halo + [up, down] + sum([piece.copies for piece in pieces], []):
                copy.sent()

    probe_out[...] = probes[OUTER]


def per_device(stripes, tiles, positions, row_offsets, amplitudes, object_field, probe_field):
    patterns, size = amplitudes.shape[1], probe_field.shape[-1]
    own_rows, own_columns = object_field.shape[1:]
    forward, inverse = dft_blocks(size)
    passes = INNER * OUTER
    pairs = stripes // 2
    half_rows = size // 2
    tile_rows = half_rows // tiles
    z_rows = tile_rows // pairs
    if not (z_rows >= 8 and z_rows * pairs == tile_rows):
        z_rows = tile_rows
    count = 8 + (passes - 1) * 12 + 4 + OUTER * (2 + 2 * (tiles - 1) + 2 * (pairs - 1) + tiles + pairs - 1)
    f32, bf16 = jnp.float32, jnp.bfloat16
    vmem = pl.BlockSpec(memory_space=pltpu.VMEM)
    return pl.pallas_call(
        functools.partial(kernel, stripes, tiles, patterns),
        out_shape=(
            jax.ShapeDtypeStruct(object_field.shape, f32),
            jax.ShapeDtypeStruct(probe_field.shape, f32),
        ),
        in_specs=[pl.BlockSpec(memory_space=pltpu.SMEM)] + [pl.BlockSpec(memory_space=pltpu.HBM)] * 5,
        out_specs=(vmem, vmem),
        scratch_shapes=[
            pltpu.VMEM(amplitudes.shape, f32),
            pltpu.VMEM(object_field.shape, f32),
            pltpu.VMEM(forward.shape, bf16),
            pltpu.VMEM(inverse.shape, bf16),
            pltpu.VMEM((2, 2, own_rows, own_columns), f32),
            pltpu.VMEM((2, 2, own_rows, own_columns), f32),
            pltpu.VMEM((2, own_rows + 2 * HALO, size), f32),
            pltpu.VMEM((2, own_rows + 2 * HALO, size), f32),
            pltpu.VMEM((2, size, size), f32),
            pltpu.VMEM((2, size, size), f32),
            pltpu.VMEM((2 * size, size), bf16),
            pltpu.VMEM((2 * size, size), bf16),
            pltpu.VMEM((passes - 1, 2, 2, own_rows, size // 2), f32),
            pltpu.VMEM((passes, 2, 2, HALO, size), f32),
            pltpu.VMEM((3, size, size), f32),
            pltpu.VMEM((OUTER + 1, 2, size, size), f32),
            pltpu.VMEM((OUTER, 3, half_rows, size), f32),
            pltpu.VMEM((3, half_rows, size), f32),
            pltpu.VMEM((OUTER, tiles - 1, 3, tile_rows, size), f32),
            pltpu.VMEM((3, tile_rows, size), f32),
            pltpu.VMEM((OUTER, pairs - 1, 3, z_rows, size), f32),
            pltpu.SemaphoreType.DMA((5,)),
            pltpu.SemaphoreType.DMA((count,)),
            pltpu.SemaphoreType.DMA((count,)),
        ],
        compiler_params=pltpu.CompilerParams(
            collective_id=0, has_side_effects=True, vmem_limit_bytes=64 * 1024 * 1024
        ),
        name="refine",
    )(row_offsets, amplitudes, object_field, probe_field, jnp.asarray(forward), jnp.asarray(inverse))


def solution(mesh):
    placed = (
        P("stripe", "tile"),
        P("stripe", "tile"),
        P("stripe", "tile", None, None),
        P(None, "stripe", "tile"),
        P(),
    )
    return jax.shard_map(
        functools.partial(per_device, mesh.shape["stripe"], mesh.shape["tile"]),
        mesh=mesh,
        in_specs=placed,
        out_specs=(P(None, "stripe", "tile"), P()),
        check_vma=False,
    )
```
